256 devices in a mesh: chan: 64 (over x, y_lo, z), win: 4 (over y_hi, core).
Axes of the slice: x: 4, y: 4 (y_hi: 2, y_lo: 2; y = y_hi * 2 + y_lo), z: 8, core: 2. Of those that a mesh axis runs over, the one named last changes fastest.
Arguments:
- traces: bfloat16 [1024, 192, 1500], P('chan', 'win'), may hold values from -6 to 6
- source_index: int32 [64], replicated, may hold values from 0 to 1023
Outputs:
- stack: float32 [2, 64, 1024, 256], P(None, 'win', 'chan')
The draws below stay inside these ranges and needn't reach their ends.
All inputs are finite; a program needn't handle non-finite values.
Results may differ from the reference program's by a relative error of at most 0.0058.
Values may be sent and summed in bfloat16 or wider, within the bound.
A program may use at most 64 MiB of HBM per device.

```python
import math
import jax
import jax.numpy as jnp
from jax import lax

CH_DEV = 16
L = 1500
F = 256
F0 = 1
K = 64
GAUGE = 4
S = 64
C = 1024
W = 192


def set_ends(array, rng, smallest, largest):
    place = [jax.random.randint(jax.random.fold_in(rng, axis), (), 0, length) for axis, length in enumerate(array.shape)]
    longest = array.shape.index(max(array.shape))
    neighbour = place[:longest] + [(place[longest] + 1) % array.shape[longest]] + place[longest + 1:]
    return array.at[tuple(place)].set(smallest).at[tuple(neighbour)].set(largest)


def block_levels(own_key, shape, cuts, low, high):
    loudness, own = 1.0, jax.random.fold_in(own_key, 6)
    for dim, blocks in cuts:
        heights = jnp.exp(jax.random.uniform(jax.random.fold_in(own, dim), (blocks,), jnp.float32, low / len(cuts), high / len(cuts)))
        loudness = loudness * jnp.repeat(heights, shape[dim] // blocks).reshape([-1 if axis == dim else 1 for axis in range(len(shape))])
    return loudness


def gaussian(stream_key, dims, deviation, most, shards=(), kind=jnp.bfloat16):
    values = deviation * jax.random.normal(stream_key, dims, jnp.float32)
    if shards:
        values = values * block_levels(stream_key, dims, shards, -0.22, 0.18)
    return jnp.clip(values, -most, most).astype(kind)


def setup_inputs(seed: int = 0) -> dict:
    key_list = jax.random.split(jax.random.key(seed), 3)
    traces = gaussian(key_list[0], (C, W, L), 1.0, 6.0, ((0, 64), (1, 4)))
    source_index = set_ends(jax.random.randint(key_list[1], (S,), 0, C), jax.random.fold_in(key_list[1], 1), 0, C - 1).astype(jnp.int32)
    return {"traces": traces, "source_index": source_index}


def make_table():
    times = jnp.arange(L, dtype=jnp.int32)[:, None]
    bins = jnp.arange(F, dtype=jnp.int32)[None, :] + F0
    phase = (times * bins % L).astype(jnp.float32) * (2.0 * math.pi / L)
    return jnp.concatenate([jnp.cos(phase), -jnp.sin(phase)], axis=1).astype(jnp.bfloat16)

def make_band():
    rows = jnp.arange(F, dtype=jnp.int32)[:, None]
    cols = jnp.arange(F, dtype=jnp.int32)[None, :]
    band = (jnp.abs(rows - cols) <= K).astype(jnp.float32)
    return (band, lax.optimization_barrier(jnp.sum(band, axis=0)))

def whiten(block, upper, table, band, counts):
    ext = jnp.concatenate([block, upper], axis=0).astype(jnp.float32)
    diff = ext[GAUGE:] - ext[:-GAUGE]
    scale = jnp.sqrt(lax.optimization_barrier(jnp.mean(diff * diff, axis=2, keepdims=True)) + 1e-05)
    normed = (diff / scale).astype(jnp.bfloat16)
    rows = normed.shape[0] * normed.shape[1]
    spec = jnp.dot(normed.reshape(rows, L).astype(jnp.float32), table.astype(jnp.float32), precision=lax.Precision.HIGHEST)
    real_part = spec[:, :F]
    imag_part = spec[:, F:]
    magnitude = jnp.sqrt(real_part * real_part + imag_part * imag_part)
    smooth = jnp.dot(magnitude, band, precision=lax.Precision.HIGHEST) / counts
    shape = (normed.shape[0], normed.shape[1], F)
    white_re = (real_part / (smooth + 1e-06)).astype(jnp.bfloat16).reshape(shape)
    white_im = (imag_part / (smooth + 1e-06)).astype(jnp.bfloat16).reshape(shape)
    return (white_re, white_im)

def reference(traces, source_index):
    table = make_table()
    band, counts = make_band()
    blocks = C // CH_DEV

    def one_block(index):
        block = lax.dynamic_slice_in_dim(traces, index * CH_DEV, CH_DEV, 0)
        start = jnp.minimum(index * CH_DEV + CH_DEV, C - GAUGE).astype(jnp.int32)
        upper = lax.dynamic_slice_in_dim(traces, start, GAUGE, 0)
        upper = jnp.where(index < blocks - 1, upper, jnp.zeros_like(upper))
        return whiten(block, upper, table, band, counts)
    white_re, white_im = lax.map(one_block, jnp.arange(blocks, dtype=jnp.int32))
    white_re = white_re.reshape(C, W, F)
    white_im = white_im.reshape(C, W, F)
    source_re = white_re[source_index].astype(jnp.float32)
    source_im = white_im[source_index].astype(jnp.float32)

    def correlate(index):
        chan_re = lax.dynamic_slice_in_dim(white_re, index * CH_DEV, CH_DEV, 0).astype(jnp.float32)
        chan_im = lax.dynamic_slice_in_dim(white_im, index * CH_DEV, CH_DEV, 0).astype(jnp.float32)
        real_out = jnp.einsum('swf,cwf->scf', source_re, chan_re) + jnp.einsum('swf,cwf->scf', source_im, chan_im)
        imag_out = jnp.einsum('swf,cwf->scf', source_im, chan_re) - jnp.einsum('swf,cwf->scf', source_re, chan_im)
        return jnp.stack([real_out, imag_out]) * (1.0 / W)
    parts = lax.map(correlate, jnp.arange(blocks, dtype=jnp.int32))
    return jnp.transpose(parts, (1, 2, 0, 3, 4)).reshape(2, S, C, F)
```

```python
import functools
import math

import jax
import jax.numpy as jnp
import ml_dtypes
import numpy as np
from jax import lax
from jax.experimental import pallas as pl
from jax.experimental.pallas import tpu as pltpu
from jax.sharding import PartitionSpec as P

F = 256
F0 = 1
K = 64
GAUGE = 4
MESH = pl.DeviceIdType.MESH
BF16 = jnp.bfloat16
F32 = jnp.float32
NT = (((1,), (1,)), ((), ()))


def make_table(length):
    times = np.arange(length, dtype=np.int64)[None, :]
    bins = np.arange(F, dtype=np.int64)[:, None] + F0
    phase = (times * bins % length).astype(np.float32) * np.float32(2.0 * math.pi / length)
    phase = phase.astype(np.float64)
    return np.concatenate([np.cos(phase), -np.sin(phase)], axis=0).astype(np.float32).astype(ml_dtypes.bfloat16)


def make_band():
    rows = np.arange(F)[:, None]
    cols = np.arange(F)[None, :]
    return (np.abs(rows - cols) <= K).astype(ml_dtypes.bfloat16)


def body(n, sizes, index_ref, traces, table, band, out_ref, prev, nxt, norm_buf, mixed, sent, held, acc, core_out, core_in,
         y_out, y_in, back_out, back_in, back_f32, halves, halo_send, halo_recv, a2a_send, a2a_recv, core_send, core_recv,
         y_send, y_recv, back_send, back_recv):
    chans, wins, length, groups, parts = sizes
    side = GAUGE // 2
    gw = wins // groups
    me = lax.axis_index("chan")
    win = lax.axis_index("win")
    core_peer = win + 1 - 2 * lax.rem(win, 2)
    y_peer = lax.rem(win + 2, 4)
    right, left = lax.rem(me + 1, n), lax.rem(me + n - 1, n)

    barrier = pltpu.get_barrier_semaphore()

    def greet(d, carry):
        pl.semaphore_signal(barrier, inc=1, device_id={"chan": lax.rem(me + d, n)}, device_id_type=MESH)
        return carry

    lax.fori_loop(1, n, greet, 0)
    pl.semaphore_signal(barrier, inc=1, device_id={"win": core_peer}, device_id_type=MESH)
    pl.semaphore_signal(barrier, inc=1, device_id={"win": y_peer}, device_id_type=MESH)
    pl.semaphore_wait(barrier, n + 1)

    def halo(g, way):
        at = pl.ds(pl.multiple_of(g * gw, gw), gw)
        if way == 0:
            return pltpu.make_async_remote_copy(
                src_ref=traces.at[pl.ds(0, side), at], dst_ref=nxt.at[:, at], send_sem=halo_send.at[g, 0],
                recv_sem=halo_recv.at[g, 0], device_id={"chan": left}, device_id_type=MESH)
        return pltpu.make_async_remote_copy(
            src_ref=traces.at[pl.ds(chans - side, side), at], dst_ref=prev.at[:, at], send_sem=halo_send.at[g, 1],
            recv_sem=halo_recv.at[g, 1], device_id={"chan": right}, device_id_type=MESH)

    for g in range(groups):
        for way in range(2):
            halo(g, way).start()

    bins = lax.broadcasted_iota(jnp.int32, (F, 1), 0)
    counts = jnp.minimum(bins + K, F - 1) - jnp.maximum(bins - K, 0) + 1
    per_count = 1.0 / counts.astype(F32)
    lane = lax.broadcasted_iota(jnp.int32, (n, 128), 1)

    def whiten(g, carry):
        at = pl.ds(pl.multiple_of(g * gw, gw), gw)
        halo(g, 0).wait()
        halo(g, 1).wait()
        for i in range(chans):
            if i < side:
                low = prev[i, at, :].astype(F32)
            else:
                low = traces[i - side, at, :].astype(F32)
            j = i + GAUGE - side
            if j < chans:
                high = traces[j, at, :].astype(F32)
                if i < side:
                    high = jnp.where(me == 0, 0.0, high)
            else:
                high = jnp.where(me == n - 1, 0.0, nxt[j - chans, at, :].astype(F32))
            diff = high - low
            scale = lax.rsqrt(jnp.sum(diff * diff, axis=1, keepdims=True) * (1.0 / length) + 1e-05)
            norm_buf[pl.ds(i * gw, gw), :] = (diff * scale).astype(BF16)
        normed = norm_buf[...]
        re = lax.dot_general(table[pl.ds(0, F), :], normed, NT, preferred_element_type=F32)
        im = lax.dot_general(table[pl.ds(F, F), :], normed, NT, preferred_element_type=F32)
        magnitude = jnp.sqrt(re * re + im * im).astype(BF16)
        smooth = jnp.dot(band[...], magnitude, preferred_element_type=F32) * per_count
        gain = 1.0 / (smooth + 1e-06)
        white = (re * gain, im * gain)
        for tile in range(2):
            q = [white[p % 2][(p // 2) * n:(p // 2 + 1) * n, tile * 128:(tile + 1) * 128] for p in range(8)]
            for bit in range(3):
                step = gw << bit
                upper = (lane // step) % 2 == 1
                fresh = list(q)
                for p in range(8):
                    if p & (1 << bit):
                        continue
                    a, b = q[p], q[p | (1 << bit)]
                    fresh[p] = jnp.where(upper, pltpu.roll(b, step, 1), a)
                    fresh[p | (1 << bit)] = jnp.where(upper, b, pltpu.roll(a, 128 - step, 1))
                q = fresh
            for c in range(8):
                mixed[pl.ds(tile * 8 + c, n, stride=chans), :] = q[c]
        sent[g] = mixed[...].astype(BF16).reshape(n, chans, 128)

        def send(d, c):
            peer = lax.rem(me + d, n)
            pltpu.make_async_remote_copy(
                src_ref=sent.at[g, peer], dst_ref=held.at[g, me], send_sem=a2a_send.at[g], recv_sem=a2a_recv.at[g],
                device_id={"chan": peer}, device_id_type=MESH).start()
            return c

        lax.fori_loop(1, n, send, 0)
        held[g, me] = sent[g, me]
        return carry

    lax.fori_loop(0, groups, whiten, 0)

    per_tile = 16
    row_tiles = []
    sub = lax.broadcasted_iota(jnp.int32, (8, 1), 0)
    owners = (win, y_peer, core_peer, lax.rem(core_peer + 2, 4))
    column = lax.broadcasted_iota(jnp.int32, (8, n * chans), 1)
    for t in range(4):
        for half in range(per_tile // 8):
            ids = jnp.zeros((8, 1), jnp.int32)
            for r in range(8):
                ids = jnp.where(sub == r, index_ref[owners[t] * per_tile + half * 8 + r], ids)
            ids = lax.rem(ids + side, n * chans)
            row_tiles.append((column == ids).astype(F32))
    picker = jnp.concatenate(row_tiles, axis=0).astype(BF16)
    lane16 = lax.broadcasted_iota(jnp.int32, (per_tile, 128), 1)
    is_im = (lane16 // gw) % 2 == 1

    def all_received(g):
        return pltpu.make_async_remote_copy(
            src_ref=sent.at[g, pl.ds(0, n - 1)], dst_ref=held.at[g, pl.ds(0, n - 1)], send_sem=a2a_send.at[g],
            recv_sem=a2a_recv.at[g], device_id={"chan": right}, device_id_type=MESH)

    rows = n * chans
    part = rows // parts

    for g in range(groups):
        all_received(g).wait_recv()
        block = held[g].reshape(rows, 128)
        picked = jnp.dot(picker, block, preferred_element_type=F32)
        pieces = []
        for t in range(4):
            pk = picked[t * per_tile:(t + 1) * per_tile]
            swapped = jnp.where(is_im, -pltpu.roll(pk, gw, 1), pltpu.roll(pk, 128 - gw, 1))
            for q in range(4):
                own = (lane16 // (2 * gw)) == q
                pieces.append(jnp.where(own, pk, 0.0))
                pieces.append(jnp.where(own, swapped, 0.0))
        weights = jnp.concatenate(pieces, axis=0).astype(BF16)
        for r in range(parts):
            at = pl.ds(r * part, part)
            rows_in = held[g, pl.ds(r * (n // parts), n // parts)].reshape(part, 128)
            term = lax.dot_general(rows_in, weights, NT, preferred_element_type=F32)
            acc[at, :] = term if g == 0 else acc[at, :] + term
    acc[pl.ds(rows, 8), :] = acc[pl.ds(0, 8), :]

    def core_copy(r):
        at = pl.ds(r * part, part)
        return pltpu.make_async_remote_copy(
            src_ref=core_out.at[:, at], dst_ref=core_in.at[:, at], send_sem=core_send.at[r], recv_sem=core_recv.at[r],
            device_id={"win": core_peer}, device_id_type=MESH)

    def y_copy(r):
        at = pl.ds(r * part, part)
        return pltpu.make_async_remote_copy(
            src_ref=y_out.at[at], dst_ref=y_in.at[at], send_sem=y_send.at[r], recv_sem=y_recv.at[r],
            device_id={"win": y_peer}, device_id_type=MESH)

    for r in range(parts):
        at, shifted = pl.ds(r * part, part), pl.ds(r * part + side, part)
        core_out[0, at, :] = acc[shifted, 256:384].astype(BF16)
        core_out[1, at, :] = acc[shifted, 384:512].astype(BF16)
        core_copy(r).start()
    for r in range(parts):
        at, shifted = pl.ds(r * part, part), pl.ds(r * part + side, part)
        core_copy(r).wait_recv()
        y_out[at, :] = (acc[shifted, 128:256] + core_in[1, at, :].astype(F32)).astype(BF16)
        y_copy(r).start()
    per_part = n // parts
    for r in range(parts):
        at, shifted = pl.ds(r * part, part), pl.ds(r * part + side, part)
        y_copy(r).wait_recv()
        total = acc[shifted, 0:128] + core_in[0, at, :].astype(F32) + y_in[at, :].astype(F32)
        back_out[pl.ds(r * per_part, per_part)] = (total * (1.0 / (wins * 4))).astype(BF16).reshape(per_part, chans, 128)

        def give(d, c):
            peer = r * per_part + lax.rem(me + d, per_part)

            @pl.when(peer != me)
            def _():
                pltpu.make_async_remote_copy(
                    src_ref=back_out.at[peer], dst_ref=back_in.at[me], send_sem=back_send, recv_sem=back_recv,
                    device_id={"chan": peer}, device_id_type=MESH).start()

            return c

        lax.fori_loop(0, per_part, give, 0)
    back_in[me] = back_out[me]
    back = pltpu.make_async_remote_copy(
        src_ref=back_out.at[pl.ds(0, n - 1)], dst_ref=back_in.at[pl.ds(0, n - 1)], send_sem=back_send, recv_sem=back_recv,
        device_id={"chan": right}, device_id_type=MESH)
    back.wait_recv()
    back_f32[...] = back_in[...].reshape(rows, 128).astype(F32)
    for c in range(chans):
        flipped = back_f32[pl.ds(c, n, stride=chans), :].T
        for half in range(2):
            both = jnp.concatenate([flipped[half * 64:half * 64 + 32], flipped[half * 64 + 32:half * 64 + 64]], axis=1)
            halves[half, pl.ds(c, 32, stride=chans), :] = both
    out_ref[:, pl.ds(0, 128)] = halves[0]
    out_ref[:, pl.ds(128, 128)] = halves[1]
    for g in range(groups):
        all_received(g).wait_send()
    for r in range(parts):
        core_copy(r).wait_send()
        y_copy(r).wait_send()
    back.wait_send()


def solution(mesh):
    n = mesh.shape["chan"]

    def per_device(traces, source_index):
        chans, wins, length = traces.shape
        groups, parts = 3, 4
        gw = wins // groups
        rows = n * chans
        vmem = pl.BlockSpec(memory_space=pltpu.VMEM)
        out = pl.pallas_call(
            functools.partial(body, n, (chans, wins, length, groups, parts)),
            out_shape=jax.ShapeDtypeStruct((2 * 16 * chans, F), F32),
            in_specs=[pl.BlockSpec(memory_space=pltpu.SMEM), vmem, vmem, vmem],
            out_specs=vmem,
            scratch_shapes=[
                pltpu.VMEM((GAUGE // 2, wins, length), BF16),
                pltpu.VMEM((GAUGE // 2, wins, length), BF16),
                pltpu.VMEM((chans * gw, length), BF16),
                pltpu.VMEM((rows, 128), F32),
                pltpu.VMEM((groups, n, chans, 128), BF16),
                pltpu.VMEM((groups, n, chans, 128), BF16),
                pltpu.VMEM((rows + 8, 512), F32),
                pltpu.VMEM((2, rows, 128), BF16),
                pltpu.VMEM((2, rows, 128), BF16),
                pltpu.VMEM((rows, 128), BF16),
                pltpu.VMEM((rows, 128), BF16),
                pltpu.VMEM((n, chans, 128), BF16),
                pltpu.VMEM((n, chans, 128), BF16),
                pltpu.VMEM((rows, 128), F32),
                pltpu.VMEM((2, 2 * 16 * chans, 128), F32),
                pltpu.SemaphoreType.DMA((groups, 2)),
                pltpu.SemaphoreType.DMA((groups, 2)),
                pltpu.SemaphoreType.DMA((groups,)),
                pltpu.SemaphoreType.DMA((groups,)),
                pltpu.SemaphoreType.DMA((parts,)),
                pltpu.SemaphoreType.DMA((parts,)),
                pltpu.SemaphoreType.DMA((parts,)),
                pltpu.SemaphoreType.DMA((parts,)),
                pltpu.SemaphoreType.DMA,
                pltpu.SemaphoreType.DMA,
            ],
            compiler_params=pltpu.CompilerParams(
                collective_id=0, has_side_effects=True, vmem_limit_bytes=48 * 2**20
            ),
        )(source_index, traces, jnp.asarray(make_table(length)), jnp.asarray(make_band()))
        return out.reshape(2, 16, chans, F)

    return jax.shard_map(
        per_device,
        mesh=mesh,
        in_specs=(P("chan", "win", None), P()),
        out_specs=P(None, "win", "chan", None),
        check_vma=False,
    )
```

```python
import functools
import math

import jax
import jax.numpy as jnp
import ml_dtypes
import numpy as np
from jax import lax
from jax.experimental import pallas as pl
from jax.experimental.pallas import tpu as pltpu
from jax.sharding import PartitionSpec as P

F = 256
F0 = 1
K = 64
GAUGE = 4
MESH = pl.DeviceIdType.MESH
BF16 = jnp.bfloat16
F32 = jnp.float32
NT = (((1,), (1,)), ((), ()))


def make_table(length):
    times = np.arange(length, dtype=np.int64)[None, :]
    bins = np.arange(F, dtype=np.int64)[:, None] + F0
    phase = (times * bins % length).astype(np.float32) * np.float32(2.0 * math.pi / length)
    phase = phase.astype(np.float64)
    band = np.zeros((F, length))
    band[:, :F] = np.abs(np.arange(F)[:, None] - np.arange(F)[None, :]) <= K
    return np.concatenate([np.cos(phase), -np.sin(phase), band], axis=0).astype(np.float32).astype(ml_dtypes.bfloat16)


def make_picker(index_ref, picker, owners, rows):
    sub = lax.broadcasted_iota(jnp.int32, (8, 1), 0)
    column = lax.broadcasted_iota(jnp.int32, (8, rows), 1)
    for t, owner in enumerate(owners):
        tiles = []
        for half in range(2):
            ids = jnp.zeros((8, 1), jnp.int32)
            for r in range(8):
                ids = jnp.where(sub == r, index_ref[owner * 16 + half * 8 + r], ids)
            tiles.append((column == ids).astype(F32))
        picker[pl.ds(t * 16, 16), :] = jnp.concatenate(tiles, axis=0).astype(BF16)


def body(n, sizes, index_ref, traces_hbm, table_hbm, near_ref, far_ref, traces, table, band, picker, load_sem, prev, nxt, norm_buf,
         mixed, sent, held, other, acc, y_out, y_in, back_out, back_in, far_out, far_in, halo_send, halo_recv, a2a_send,
         a2a_recv, core_send, core_recv, y_send, y_recv, back_send, back_recv, far_send,
         far_recv, group_sem, all_sem):
    chans, wins, length, groups, parts = sizes
    side = GAUGE // 2
    gw = wins // groups
    rows = n * chans
    me = lax.axis_index("chan")
    win = lax.axis_index("win")
    core_peer = win + 1 - 2 * lax.rem(win, 2)
    y_peer = lax.rem(win + 2, 4)
    right, left = lax.rem(me + 1, n), lax.rem(me + n - 1, n)

    barrier = pltpu.get_barrier_semaphore()

    line = 8
    far_in[...] = jnp.zeros_like(far_in)
    for d in range(1, line):
        pl.semaphore_signal(
            barrier, inc=1, device_id={"chan": me // line * line + lax.rem(me + d, line)}, device_id_type=MESH)
        pl.semaphore_signal(barrier, inc=1, device_id={"chan": lax.rem(me + line * d, n)}, device_id_type=MESH)
    for peer in (left, right):
        pl.semaphore_signal(barrier, inc=1, device_id={"chan": peer}, device_id_type=MESH)
    for peer in (core_peer, y_peer):
        pl.semaphore_signal(barrier, inc=1, device_id={"win": peer}, device_id_type=MESH)

    def load(g):
        at = pl.ds(g * gw, gw)
        return pltpu.make_async_copy(traces_hbm.at[:, at], traces.at[:, at], load_sem.at[g])

    load_table = pltpu.make_async_copy(table_hbm.at[pl.ds(0, 2 * F)], table, load_sem.at[groups])
    load_band = pltpu.make_async_copy(table_hbm.at[pl.ds(2 * F, F), pl.ds(0, F)], band, load_sem.at[groups + 1])
    load(0).start()
    load_table.start()
    load_band.start()
    for g in range(1, groups):
        load(g).start()
    make_picker(index_ref, picker, (win, y_peer), rows)
    pl.semaphore_wait(barrier, 2 * line + 2)

    def halo(g, way):
        at = pl.ds(pl.multiple_of(g * gw, gw), gw)
        if way == 0:
            return pltpu.make_async_remote_copy(
                src_ref=traces_hbm.at[pl.ds(0, side), at], dst_ref=nxt.at[:, at], send_sem=halo_send.at[g, 0],
                recv_sem=halo_recv.at[g, 0], device_id={"chan": left}, device_id_type=MESH)
        return pltpu.make_async_remote_copy(
            src_ref=traces_hbm.at[pl.ds(chans - side, side), at], dst_ref=prev.at[:, at], send_sem=halo_send.at[g, 1],
            recv_sem=halo_recv.at[g, 1], device_id={"chan": right}, device_id_type=MESH)

    for g in range(groups):
        for way in range(2):
            halo(g, way).start()
    for d in range(1, line):
        pl.semaphore_signal(
            group_sem, inc=1, device_id={"chan": me // line * line + lax.rem(me + d, line)}, device_id_type=MESH)
    load_table.wait()
    load_band.wait()
    for g in range(groups):
        load(g).wait()

    bins = lax.broadcasted_iota(jnp.int32, (F, 1), 0)
    counts = jnp.minimum(bins + K, F - 1) - jnp.maximum(bins - K, 0) + 1
    per_count = 1.0 / counts.astype(F32)
    lane = lax.broadcasted_iota(jnp.int32, (n, 128), 1)

    def normalise(g, i):
        at = pl.ds(pl.multiple_of(g * gw, gw), gw)
        if i < chans - side:
            low = traces[i, at, :].astype(F32)
            if i + GAUGE < chans:
                high = traces[i + GAUGE, at, :].astype(F32)
            else:
                high = jnp.where(me == n - 1, 0.0, nxt[i + GAUGE - chans, at, :].astype(F32))
        else:
            low = prev[i - chans + side, at, :].astype(F32)
            high = jnp.where(me == 0, 0.0, traces[i - chans + GAUGE, at, :].astype(F32))
        diff = high - low
        scale = lax.rsqrt(jnp.sum(diff * diff, axis=1, keepdims=True) * (1.0 / length) + 1e-05)
        norm_buf[g, pl.ds(i * gw, gw), :] = (diff * scale).astype(BF16)

    def whiten(g, tile):
        normed = norm_buf[g, pl.ds(tile * 128, 128), :]
        re = lax.dot_general(table[pl.ds(0, F), :], normed, NT, preferred_element_type=F32)
        im = lax.dot_general(table[pl.ds(F, F), :], normed, NT, preferred_element_type=F32)
        magnitude = jnp.sqrt(re * re + im * im).astype(BF16)
        smooth = jnp.dot(band[...], magnitude, preferred_element_type=F32) * per_count
        gain = 1.0 / (smooth + 1e-06)
        white = (re * gain, im * gain)
        q = [white[p % 2][(p // 2) * n:(p // 2 + 1) * n] for p in range(8)]
        for bit in range(3):
            step = gw << bit
            upper = (lane // step) % 2 == 1
            fresh = list(q)
            for p in range(8):
                if p & (1 << bit):
                    continue
                a, b = q[p], q[p | (1 << bit)]
                fresh[p] = jnp.where(upper, pltpu.roll(b, step, 1), a)
                fresh[p | (1 << bit)] = jnp.where(upper, b, pltpu.roll(a, 128 - step, 1))
            q = fresh
        for c in range(8):
            mixed[g, pl.ds(tile * 8 + c, n, stride=chans), :] = q[c]

    def before(g, carry):
        for i in range(chans - GAUGE):
            normalise(g, i)
        whiten(g, 0)
        return carry

    lax.fori_loop(0, groups, before, 0)
    pl.semaphore_wait(group_sem, line - 1)
    pl.semaphore_signal(all_sem, inc=1, device_id={"win": y_peer}, device_id_type=MESH)

    def after(g, carry):
        halo(g, 0).wait()
        halo(g, 1).wait()
        for i in range(chans - GAUGE, chans):
            normalise(g, i)
        whiten(g, 1)
        sent[g] = mixed[g].astype(BF16).reshape(n, chans, 128)

        def send(d, c):
            peer = lax.rem(me + d, n)
            pltpu.make_async_remote_copy(
                src_ref=sent.at[g, peer], dst_ref=held.at[g, me], send_sem=a2a_send.at[g], recv_sem=a2a_recv.at[g],
                device_id={"chan": peer}, device_id_type=MESH).start()
            return c

        lax.fori_loop(1, n, send, 0)
        held[g, me] = sent[g, me]
        return carry

    lax.fori_loop(0, groups, after, 0)

    def all_received(g):
        return pltpu.make_async_remote_copy(
            src_ref=sent.at[g, pl.ds(0, n - 1)], dst_ref=held.at[g, pl.ds(0, n - 1)], send_sem=a2a_send.at[g],
            recv_sem=a2a_recv.at[g], device_id={"chan": right}, device_id_type=MESH)

    def forward(g):
        return pltpu.make_async_remote_copy(
            src_ref=held.at[g], dst_ref=other.at[g], send_sem=core_send.at[g], recv_sem=core_recv.at[g],
            device_id={"win": core_peer}, device_id_type=MESH)

    lane16 = lax.broadcasted_iota(jnp.int32, (16, 128), 1)
    is_im = (lane16 // gw) % 2 == 1
    own_row = lax.broadcasted_iota(jnp.int32, (n, chans, 128), 1) < chans - side

    def straight(block):
        block = block.astype(F32)
        following = jnp.concatenate([block[1:], block[:1]], axis=0)
        return jnp.where(own_row, block, following).reshape(rows, 128).astype(BF16)

    def weights_of(block):
        picked = jnp.dot(picker[...], block, preferred_element_type=F32)
        pieces = []
        for t in range(2):
            pk = picked[t * 16:(t + 1) * 16]
            swapped = jnp.where(is_im, -pltpu.roll(pk, gw, 1), pltpu.roll(pk, 128 - gw, 1))
            for q in range(4):
                mine = (lane16 // (2 * gw)) == q
                pieces.append(jnp.where(mine, pk, 0.0))
                pieces.append(jnp.where(mine, swapped, 0.0))
        return jnp.concatenate(pieces, axis=0).astype(BF16)

    blocks, weights = [], []
    for g in range(groups):
        all_received(g).wait_recv()
        forward(g).start()
        for source in (held, other):
            if source is other:
                forward(g).wait_recv()
            blocks.append(straight(source[g]))
            weights.append(weights_of(blocks[-1]))
        block = jnp.concatenate(blocks[-2:], axis=1)
        weight = jnp.concatenate(weights[-2:], axis=1)
        term = lax.dot_general(block, weight, NT, preferred_element_type=F32)
        if g == 0:
            acc[...] = term
        else:
            acc[...] += term

    part = rows // parts
    per_part = n // parts
    first_peer = me // (n // 4) * (n // 4)

    def base(r):
        return lax.rem(first_peer + r * per_part, n)

    def at(r):
        return pl.ds(pl.multiple_of(base(r) * chans, part), part)

    def y_copy(r):
        return pltpu.make_async_remote_copy(
            src_ref=y_out.at[at(r)], dst_ref=y_in.at[at(r)], send_sem=y_send.at[r], recv_sem=y_recv.at[r],
            device_id={"win": y_peer}, device_id_type=MESH)

    summed = [r for r in range(parts) if r // (parts // 4) % 2 == 0]
    direct = [r for r in range(parts) if r not in summed]
    share = 1.0 / (wins * 4)

    def give(r, source, target, to_win, sems, skip):
        def one(d, c):
            peer = base(r) + lax.rem(me + d, per_part)

            def start():
                pltpu.make_async_remote_copy(
                    src_ref=source.at[peer], dst_ref=target.at[me], send_sem=sems[0], recv_sem=sems[1],
                    device_id={"chan": peer, "win": to_win}, device_id_type=MESH).start()

            if skip:
                pl.when(peer != me)(start)
            else:
                start()
            return c

        lax.fori_loop(0, per_part, one, 0)

    def tiles(value):
        return (value * share).astype(BF16).reshape(per_part, chans, 128)

    for r in summed:
        y_out[at(r), :] = acc[at(r), 128:256].astype(BF16)
        y_copy(r).start()
    pl.semaphore_wait(all_sem, 1)
    for r in direct:
        back_out[pl.ds(base(r), per_part)] = tiles(acc[at(r), 0:128])
        give(r, back_out, back_in, win, (back_send, back_recv), False)
        far_out[pl.ds(base(r), per_part)] = tiles(acc[at(r), 128:256])
        give(r, far_out, far_in, y_peer, (far_send, far_recv), False)
    for r in summed:
        y_copy(r).wait_recv()
        back_out[pl.ds(base(r), per_part)] = tiles(acc[at(r), 0:128] + y_in[at(r), :].astype(F32))
        give(r, back_out, back_in, win, (back_send, back_recv), r // (parts // 4) == 0)
    back_in[me] = back_out[me]

    def all_back(source, target, count, sems):
        return pltpu.make_async_remote_copy(
            src_ref=source.at[pl.ds(0, count)], dst_ref=target.at[pl.ds(0, count)], send_sem=sems[0], recv_sem=sems[1],
            device_id={"chan": right}, device_id_type=MESH)

    back = all_back(back_out, back_in, n - 1, (back_send, back_recv))
    far = all_back(far_out, far_in, n // 2, (far_send, far_recv))
    back.wait_recv()
    far.wait_recv()
    near_ref[...] = back_in[...]
    far_ref[...] = far_in[...]
    for g in range(groups):
        all_received(g).wait_send()
        forward(g).wait_send()
    for r in summed:
        y_copy(r).wait_send()
    back.wait_send()
    far.wait_send()


def arrange(near, far, out_ref, back_f32, halves):
    n, chans, _ = near.shape
    back_f32[...] = (near[...].astype(F32) + far[...].astype(F32)).reshape(n * chans, 128)
    for c in range(chans):
        flipped = back_f32[pl.ds(c, n, stride=chans), :].T
        for half in range(2):
            both = jnp.concatenate([flipped[half * 64:half * 64 + 32], flipped[half * 64 + 32:half * 64 + 64]], axis=1)
            halves[half, pl.ds(c, 32, stride=chans), :] = both
    out_ref[:, pl.ds(0, 128)] = halves[0]
    out_ref[:, pl.ds(128, 128)] = halves[1]


def solution(mesh):
    n = mesh.shape["chan"]

    def per_device(traces, source_index):
        chans, wins, length = traces.shape
        groups, parts = 3, 8
        gw = wins // groups
        rows = n * chans
        vmem = pl.BlockSpec(memory_space=pltpu.VMEM)
        hbm = pl.BlockSpec(memory_space=pltpu.HBM)
        near, far = pl.pallas_call(
            functools.partial(body, n, (chans, wins, length, groups, parts)),
            out_shape=[jax.ShapeDtypeStruct((n, chans, 128), BF16)] * 2,
            in_specs=[pl.BlockSpec(memory_space=pltpu.SMEM), hbm, hbm],
            out_specs=[vmem, vmem],
            scratch_shapes=[
                pltpu.VMEM((chans, wins, length), BF16),
                pltpu.VMEM((2 * F, length), BF16),
                pltpu.VMEM((F, F), BF16),
                pltpu.VMEM((2 * 16, rows), BF16),
                pltpu.SemaphoreType.DMA((groups + 2,)),
                pltpu.VMEM((GAUGE // 2, wins, length), BF16),
                pltpu.VMEM((GAUGE // 2, wins, length), BF16),
                pltpu.VMEM((groups, chans * gw, length), BF16),
                pltpu.VMEM((groups, rows, 128), F32),
                pltpu.VMEM((groups, n, chans, 128), BF16),
                pltpu.VMEM((groups, n, chans, 128), BF16),
                pltpu.VMEM((groups, n, chans, 128), BF16),
                pltpu.VMEM((rows, 256), F32),
                pltpu.VMEM((rows, 128), BF16),
                pltpu.VMEM((rows, 128), BF16),
                pltpu.VMEM((n, chans, 128), BF16),
                pltpu.VMEM((n, chans, 128), BF16),
                pltpu.VMEM((n, chans, 128), BF16),
                pltpu.VMEM((n, chans, 128), BF16),
                pltpu.SemaphoreType.DMA((groups, 2)),
                pltpu.SemaphoreType.DMA((groups, 2)),
                pltpu.SemaphoreType.DMA((groups,)),
                pltpu.SemaphoreType.DMA((groups,)),
                pltpu.SemaphoreType.DMA((groups,)),
                pltpu.SemaphoreType.DMA((groups,)),
                pltpu.SemaphoreType.DMA((parts,)),
                pltpu.SemaphoreType.DMA((parts,)),
                pltpu.SemaphoreType.DMA,
                pltpu.SemaphoreType.DMA,
                pltpu.SemaphoreType.DMA,
                pltpu.SemaphoreType.DMA,
                pltpu.SemaphoreType.REGULAR,
                pltpu.SemaphoreType.REGULAR,
            ],
            compiler_params=pltpu.CompilerParams(
                collective_id=0, has_side_effects=True, vmem_limit_bytes=62 * 2**20
            ),
        )(source_index, traces, jnp.asarray(make_table(length)))
        out = pl.pallas_call(
            arrange,
            out_shape=jax.ShapeDtypeStruct((2 * 16 * chans, F), F32),
            in_specs=[vmem, vmem],
            out_specs=vmem,
            scratch_shapes=[pltpu.VMEM((rows, 128), F32), pltpu.VMEM((2, 2 * 16 * chans, 128), F32)],
        )(near, far)
        return out.reshape(2, 16, chans, F)

    return jax.shard_map(
        per_device,
        mesh=mesh,
        in_specs=(P("chan", "win", None), P()),
        out_specs=P(None, "win", "chan", None),
        check_vma=False,
    )
```

```python
import functools
import math

import jax
import jax.numpy as jnp
import ml_dtypes
import numpy as np
from jax import lax
from jax.experimental import pallas as pl
from jax.experimental.pallas import tpu as pltpu
from jax.sharding import PartitionSpec as P

F = 256
F0 = 1
K = 64
GAUGE = 4
MESH = pl.DeviceIdType.MESH
BF16 = jnp.bfloat16
F32 = jnp.float32
NT = (((1,), (1,)), ((), ()))


def make_table(length):
    times = np.arange(length, dtype=np.int64)[None, :]
    bins = np.arange(F, dtype=np.int64)[:, None] + F0
    phase = (times * bins % length).astype(np.float32) * np.float32(2.0 * math.pi / length)
    phase = phase.astype(np.float64)
    band = np.zeros((F, length))
    band[:, :F] = np.abs(np.arange(F)[:, None] - np.arange(F)[None, :]) <= K
    return np.concatenate([np.cos(phase), -np.sin(phase), band], axis=0).astype(np.float32).astype(ml_dtypes.bfloat16)


def make_picker(index_ref, picker, owners, rows):
    sub = lax.broadcasted_iota(jnp.int32, (8, 1), 0)
    column = lax.broadcasted_iota(jnp.int32, (8, rows), 1)
    for t, owner in enumerate(owners):
        tiles = []
        for half in range(2):
            ids = jnp.zeros((8, 1), jnp.int32)
            for r in range(8):
                ids = jnp.where(sub == r, index_ref[owner * 16 + half * 8 + r], ids)
            tiles.append((column == ids).astype(F32))
        picker[pl.ds(t * 16, 16), :] = jnp.concatenate(tiles, axis=0).astype(BF16)


def body(n, sizes, index_ref, traces_hbm, table_hbm, out_ref, traces, table, band, picker, load_sem, prev, nxt, norm_buf,
         mixed, sent, held, other, acc, y_out, y_in, back_out, back_in, far_out, far_in, halo_send, halo_recv, a2a_send,
         a2a_recv, core_send, core_recv, y_send, y_recv, back_send, back_recv, far_send,
         far_recv, group_sem, all_sem, back_f32, halves):
    chans, wins, length, groups, parts = sizes
    side = GAUGE // 2
    gw = wins // groups
    rows = n * chans
    me = lax.axis_index("chan")
    win = lax.axis_index("win")
    core_peer = win + 1 - 2 * lax.rem(win, 2)
    y_peer = lax.rem(win + 2, 4)
    right, left = lax.rem(me + 1, n), lax.rem(me + n - 1, n)

    barrier = pltpu.get_barrier_semaphore()

    line = 8
    far_in[...] = jnp.zeros_like(far_in)
    for d in range(1, line):
        pl.semaphore_signal(
            barrier, inc=1, device_id={"chan": me // line * line + lax.rem(me + d, line)}, device_id_type=MESH)
        pl.semaphore_signal(barrier, inc=1, device_id={"chan": lax.rem(me + line * d, n)}, device_id_type=MESH)
    for peer in (left, right):
        pl.semaphore_signal(barrier, inc=1, device_id={"chan": peer}, device_id_type=MESH)
    for peer in (core_peer, y_peer):
        pl.semaphore_signal(barrier, inc=1, device_id={"win": peer}, device_id_type=MESH)

    def load(g):
        at = pl.ds(g * gw, gw)
        return pltpu.make_async_copy(traces_hbm.at[:, at], traces.at[:, at], load_sem.at[g])

    load_table = pltpu.make_async_copy(table_hbm.at[pl.ds(0, 2 * F)], table, load_sem.at[groups])
    load_band = pltpu.make_async_copy(table_hbm.at[pl.ds(2 * F, F), pl.ds(0, F)], band, load_sem.at[groups + 1])
    load(0).start()
    load_table.start()
    load_band.start()
    for g in range(1, groups):
        load(g).start()
    make_picker(index_ref, picker, (win, y_peer), rows)
    pl.semaphore_wait(barrier, 2 * line + 2)

    def halo(g, way):
        at = pl.ds(pl.multiple_of(g * gw, gw), gw)
        if way == 0:
            return pltpu.make_async_remote_copy(
                src_ref=traces_hbm.at[pl.ds(0, side), at], dst_ref=nxt.at[:, at], send_sem=halo_send.at[g, 0],
                recv_sem=halo_recv.at[g, 0], device_id={"chan": left}, device_id_type=MESH)
        return pltpu.make_async_remote_copy(
            src_ref=traces_hbm.at[pl.ds(chans - side, side), at], dst_ref=prev.at[:, at], send_sem=halo_send.at[g, 1],
            recv_sem=halo_recv.at[g, 1], device_id={"chan": right}, device_id_type=MESH)

    for g in range(groups):
        for way in range(2):
            halo(g, way).start()
    for d in range(1, line):
        pl.semaphore_signal(
            group_sem, inc=1, device_id={"chan": me // line * line + lax.rem(me + d, line)}, device_id_type=MESH)
    load_table.wait()
    load_band.wait()
    for g in range(groups):
        load(g).wait()

    bins = lax.broadcasted_iota(jnp.int32, (F, 1), 0)
    counts = jnp.minimum(bins + K, F - 1) - jnp.maximum(bins - K, 0) + 1
    per_count = 1.0 / counts.astype(F32)
    lane = lax.broadcasted_iota(jnp.int32, (n, 128), 1)

    def normalise(g, i):
        at = pl.ds(pl.multiple_of(g * gw, gw), gw)
        if i < chans - side:
            low = traces[i, at, :].astype(F32)
            if i + GAUGE < chans:
                high = traces[i + GAUGE, at, :].astype(F32)
            else:
                high = jnp.where(me == n - 1, 0.0, nxt[i + GAUGE - chans, at, :].astype(F32))
        else:
            low = prev[i - chans + side, at, :].astype(F32)
            high = jnp.where(me == 0, 0.0, traces[i - chans + GAUGE, at, :].astype(F32))
        diff = high - low
        scale = lax.rsqrt(jnp.sum(diff * diff, axis=1, keepdims=True) * (1.0 / length) + 1e-05)
        norm_buf[g, pl.ds(i * gw, gw), :] = (diff * scale).astype(BF16)

    def whiten(g, tile):
        normed = norm_buf[g, pl.ds(tile * 128, 128), :]
        re = lax.dot_general(table[pl.ds(0, F), :], normed, NT, preferred_element_type=F32)
        im = lax.dot_general(table[pl.ds(F, F), :], normed, NT, preferred_element_type=F32)
        magnitude = jnp.sqrt(re * re + im * im).astype(BF16)
        smooth = jnp.dot(band[...], magnitude, preferred_element_type=F32) * per_count
        gain = 1.0 / (smooth + 1e-06)
        white = (re * gain, im * gain)
        q = [white[p % 2][(p // 2) * n:(p // 2 + 1) * n] for p in range(8)]
        for bit in range(3):
            step = gw << bit
            upper = (lane // step) % 2 == 1
            fresh = list(q)
            for p in range(8):
                if p & (1 << bit):
                    continue
                a, b = q[p], q[p | (1 << bit)]
                fresh[p] = jnp.where(upper, pltpu.roll(b, step, 1), a)
                fresh[p | (1 << bit)] = jnp.where(upper, b, pltpu.roll(a, 128 - step, 1))
            q = fresh
        for c in range(8):
            mixed[g, pl.ds(tile * 8 + c, n, stride=chans), :] = q[c]

    def before(g, carry):
        for i in range(chans - GAUGE):
            normalise(g, i)
        whiten(g, 0)
        return carry

    lax.fori_loop(0, groups, before, 0)
    pl.semaphore_wait(group_sem, line - 1)
    pl.semaphore_signal(all_sem, inc=1, device_id={"win": y_peer}, device_id_type=MESH)

    def after(g, carry):
        halo(g, 0).wait()
        halo(g, 1).wait()
        for i in range(chans - GAUGE, chans):
            normalise(g, i)
        whiten(g, 1)
        sent[g] = mixed[g].astype(BF16).reshape(n, chans, 128)

        def send(d, c):
            peer = lax.rem(me + d, n)
            pltpu.make_async_remote_copy(
                src_ref=sent.at[g, peer], dst_ref=held.at[g, me], send_sem=a2a_send.at[g], recv_sem=a2a_recv.at[g],
                device_id={"chan": peer}, device_id_type=MESH).start()
            return c

        lax.fori_loop(1, n, send, 0)
        held[g, me] = sent[g, me]
        return carry

    lax.fori_loop(0, groups, after, 0)

    def all_received(g):
        return pltpu.make_async_remote_copy(
            src_ref=sent.at[g, pl.ds(0, n - 1)], dst_ref=held.at[g, pl.ds(0, n - 1)], send_sem=a2a_send.at[g],
            recv_sem=a2a_recv.at[g], device_id={"chan": right}, device_id_type=MESH)

    def forward(g):
        return pltpu.make_async_remote_copy(
            src_ref=held.at[g], dst_ref=other.at[g], send_sem=core_send.at[g], recv_sem=core_recv.at[g],
            device_id={"win": core_peer}, device_id_type=MESH)

    lane16 = lax.broadcasted_iota(jnp.int32, (16, 128), 1)
    is_im = (lane16 // gw) % 2 == 1
    own_row = lax.broadcasted_iota(jnp.int32, (n, chans, 128), 1) < chans - side

    def straight(block):
        block = block.astype(F32)
        following = jnp.concatenate([block[1:], block[:1]], axis=0)
        return jnp.where(own_row, block, following).reshape(rows, 128).astype(BF16)

    def weights_of(block):
        picked = jnp.dot(picker[...], block, preferred_element_type=F32)
        pieces = []
        for t in range(2):
            pk = picked[t * 16:(t + 1) * 16]
            swapped = jnp.where(is_im, -pltpu.roll(pk, gw, 1), pltpu.roll(pk, 128 - gw, 1))
            for q in range(4):
                mine = (lane16 // (2 * gw)) == q
                pieces.append(jnp.where(mine, pk, 0.0))
                pieces.append(jnp.where(mine, swapped, 0.0))
        return jnp.concatenate(pieces, axis=0).astype(BF16)

    blocks, weights = [], []
    for g in range(groups):
        all_received(g).wait_recv()
        forward(g).start()
        for source in (held, other):
            if source is other:
                forward(g).wait_recv()
            blocks.append(straight(source[g]))
            weights.append(weights_of(blocks[-1]))
        block = jnp.concatenate(blocks[-2:], axis=1)
        weight = jnp.concatenate(weights[-2:], axis=1)
        term = lax.dot_general(block, weight, NT, preferred_element_type=F32)
        if g == 0:
            acc[...] = term
        else:
            acc[...] += term

    part = rows // parts
    per_part = n // parts
    first_peer = me // (n // 4) * (n // 4)

    def base(r):
        return lax.rem(first_peer + r * per_part, n)

    def at(r):
        return pl.ds(pl.multiple_of(base(r) * chans, part), part)

    def y_copy(r):
        return pltpu.make_async_remote_copy(
            src_ref=y_out.at[at(r)], dst_ref=y_in.at[at(r)], send_sem=y_send.at[r], recv_sem=y_recv.at[r],
            device_id={"win": y_peer}, device_id_type=MESH)

    summed = [r for r in range(parts) if r // (parts // 4) % 2 == 1]
    direct = [r for r in range(parts) if r not in summed]
    share = 1.0 / (wins * 4)

    def give(r, source, target, to_win, sems, skip):
        def one(d, c):
            peer = base(r) + lax.rem(me + d, per_part)

            def start():
                pltpu.make_async_remote_copy(
                    src_ref=source.at[peer], dst_ref=target.at[me], send_sem=sems[0], recv_sem=sems[1],
                    device_id={"chan": peer, "win": to_win}, device_id_type=MESH).start()

            if skip:
                pl.when(peer != me)(start)
            else:
                start()
            return c

        lax.fori_loop(0, per_part, one, 0)

    def tiles(value):
        return (value * share).astype(BF16).reshape(per_part, chans, 128)

    for r in summed:
        y_out[at(r), :] = acc[at(r), 128:256].astype(BF16)
        y_copy(r).start()
    pl.semaphore_wait(all_sem, 1)
    for r in direct:
        back_out[pl.ds(base(r), per_part)] = tiles(acc[at(r), 0:128])
        give(r, back_out, back_in, win, (back_send, back_recv), r // (parts // 4) == 0)
        far_out[pl.ds(base(r), per_part)] = tiles(acc[at(r), 128:256])
        give(r, far_out, far_in, y_peer, (far_send, far_recv), False)
    for r in summed:
        y_copy(r).wait_recv()
        back_out[pl.ds(base(r), per_part)] = tiles(acc[at(r), 0:128] + y_in[at(r), :].astype(F32))
        give(r, back_out, back_in, win, (back_send, back_recv), False)
    back_in[me] = back_out[me]

    def all_back(source, target, count, sems):
        return pltpu.make_async_remote_copy(
            src_ref=source.at[pl.ds(0, count)], dst_ref=target.at[pl.ds(0, count)], send_sem=sems[0], recv_sem=sems[1],
            device_id={"chan": right}, device_id_type=MESH)

    back = all_back(back_out, back_in, n - 1, (back_send, back_recv))
    far = all_back(far_out, far_in, n // 2, (far_send, far_recv))
    back.wait_recv()
    far.wait_recv()
    arrange(back_in, far_in, out_ref, back_f32, halves)
    for g in range(groups):
        all_received(g).wait_send()
        forward(g).wait_send()
    for r in summed:
        y_copy(r).wait_send()
    back.wait_send()
    far.wait_send()


def arrange(near, far, out_ref, back_f32, halves):
    n, chans, _ = near.shape
    back_f32[...] = (near[...].astype(F32) + far[...].astype(F32)).reshape(n * chans, 128)
    for c in range(chans):
        flipped = back_f32[pl.ds(c, n, stride=chans), :].T
        for half in range(2):
            both = jnp.concatenate([flipped[half * 64:half * 64 + 32], flipped[half * 64 + 32:half * 64 + 64]], axis=1)
            halves[half, pl.ds(c, 32, stride=chans), :] = both
    out_ref[:, pl.ds(0, 128)] = halves[0]
    out_ref[:, pl.ds(128, 128)] = halves[1]


def solution(mesh):
    n = mesh.shape["chan"]

    def per_device(traces, source_index):
        chans, wins, length = traces.shape
        groups, parts = 3, 8
        gw = wins // groups
        rows = n * chans
        vmem = pl.BlockSpec(memory_space=pltpu.VMEM)
        hbm = pl.BlockSpec(memory_space=pltpu.HBM)
        out = pl.pallas_call(
            functools.partial(body, n, (chans, wins, length, groups, parts)),
            out_shape=jax.ShapeDtypeStruct((2 * 16 * chans, F), F32),
            in_specs=[pl.BlockSpec(memory_space=pltpu.SMEM), hbm, hbm],
            out_specs=vmem,
            scratch_shapes=[
                pltpu.VMEM((chans, wins, length), BF16),
                pltpu.VMEM((2 * F, length), BF16),
                pltpu.VMEM((F, F), BF16),
                pltpu.VMEM((2 * 16, rows), BF16),
                pltpu.SemaphoreType.DMA((groups + 2,)),
                pltpu.VMEM((GAUGE // 2, wins, length), BF16),
                pltpu.VMEM((GAUGE // 2, wins, length), BF16),
                pltpu.VMEM((groups, chans * gw, length), BF16),
                pltpu.VMEM((groups, rows, 128), F32),
                pltpu.VMEM((groups, n, chans, 128), BF16),
                pltpu.VMEM((groups, n, chans, 128), BF16),
                pltpu.VMEM((groups, n, chans, 128), BF16),
                pltpu.VMEM((rows, 256), F32),
                pltpu.VMEM((rows, 128), BF16),
                pltpu.VMEM((rows, 128), BF16),
                pltpu.VMEM((n, chans, 128), BF16),
                pltpu.VMEM((n, chans, 128), BF16),
                pltpu.VMEM((n, chans, 128), BF16),
                pltpu.VMEM((n, chans, 128), BF16),
                pltpu.SemaphoreType.DMA((groups, 2)),
                pltpu.SemaphoreType.DMA((groups, 2)),
                pltpu.SemaphoreType.DMA((groups,)),
                pltpu.SemaphoreType.DMA((groups,)),
                pltpu.SemaphoreType.DMA((groups,)),
                pltpu.SemaphoreType.DMA((groups,)),
                pltpu.SemaphoreType.DMA((parts,)),
                pltpu.SemaphoreType.DMA((parts,)),
                pltpu.SemaphoreType.DMA,
                pltpu.SemaphoreType.DMA,
                pltpu.SemaphoreType.DMA,
                pltpu.SemaphoreType.DMA,
                pltpu.SemaphoreType.REGULAR,
                pltpu.SemaphoreType.REGULAR,
                pltpu.VMEM((rows, 128), F32),
                pltpu.VMEM((2, 2 * 16 * chans, 128), F32),
            ],
            compiler_params=pltpu.CompilerParams(
                collective_id=0, has_side_effects=True, vmem_limit_bytes=52 * 2**20
            ),
        )(source_index, traces, jnp.asarray(make_table(length)))
        return out.reshape(2, 16, chans, F)

    return jax.shard_map(
        per_device,
        mesh=mesh,
        in_specs=(P("chan", "win", None), P()),
        out_specs=P(None, "win", "chan", None),
        check_vma=False,
    )
```

```python
import functools
import math

import jax
import jax.numpy as jnp
import ml_dtypes
import numpy as np
from jax import lax
from jax.experimental import pallas as pl
from jax.experimental.pallas import tpu as pltpu
from jax.sharding import PartitionSpec as P

F = 256
F0 = 1
K = 64
GAUGE = 4
MESH = pl.DeviceIdType.MESH
BF16 = jnp.bfloat16
F32 = jnp.float32
NT = (((1,), (1,)), ((), ()))


def make_table(length):
    times = np.arange(length, dtype=np.int64)[None, :]
    bins = np.arange(F, dtype=np.int64)[:, None] + F0
    phase = (times * bins % length).astype(np.float32) * np.float32(2.0 * math.pi / length)
    phase = phase.astype(np.float64)
    band = np.zeros((F, length))
    band[:, :F] = np.abs(np.arange(F)[:, None] - np.arange(F)[None, :]) <= K
    return np.concatenate([np.cos(phase), -np.sin(phase), band], axis=0).astype(np.float32).astype(ml_dtypes.bfloat16)


def make_picker(index_ref, picker, owners, rows):
    sub = lax.broadcasted_iota(jnp.int32, (8, 1), 0)
    column = lax.broadcasted_iota(jnp.int32, (8, rows), 1)
    for t, owner in enumerate(owners):
        tiles = []
        for half in range(2):
            ids = jnp.zeros((8, 1), jnp.int32)
            for r in range(8):
                ids = jnp.where(sub == r, index_ref[owner * 16 + half * 8 + r], ids)
            tiles.append((column == ids).astype(F32))
        picker[pl.ds(t * 16, 16), :] = jnp.concatenate(tiles, axis=0).astype(BF16)


def body(n, sizes, index_ref, traces_hbm, table_hbm, out_ref, traces, table, band, picker, load_sem, prev, nxt, norm_buf,
         mixed, sent, held, other, acc, y_out, y_in, back_out, back_in, far_out, far_in, halo_send, halo_recv, a2a_send,
         a2a_recv, core_send, core_recv, y_send, y_recv, back_send, back_recv, far_send,
         far_recv, group_sem, all_sem, back_f32, halves):
    chans, wins, length, groups, parts = sizes
    side = GAUGE // 2
    gw = wins // groups
    rows = n * chans
    me = lax.axis_index("chan")
    win = lax.axis_index("win")
    core_peer = win + 1 - 2 * lax.rem(win, 2)
    y_peer = lax.rem(win + 2, 4)
    right, left = lax.rem(me + 1, n), lax.rem(me + n - 1, n)

    barrier = pltpu.get_barrier_semaphore()

    line = 8
    far_in[...] = jnp.zeros_like(far_in)
    for d in range(1, line):
        pl.semaphore_signal(
            barrier, inc=1, device_id={"chan": me // line * line + lax.rem(me + d, line)}, device_id_type=MESH)
        pl.semaphore_signal(barrier, inc=1, device_id={"chan": lax.rem(me + line * d, n)}, device_id_type=MESH)
    for peer in (left, right):
        pl.semaphore_signal(barrier, inc=1, device_id={"chan": peer}, device_id_type=MESH)
    for peer in (core_peer, y_peer):
        pl.semaphore_signal(barrier, inc=1, device_id={"win": peer}, device_id_type=MESH)

    def load(g):
        at = pl.ds(g * gw, gw)
        return pltpu.make_async_copy(traces_hbm.at[:, at], traces.at[:, at], load_sem.at[g])

    load_table = pltpu.make_async_copy(table_hbm.at[pl.ds(0, 2 * F)], table, load_sem.at[groups])
    load_band = pltpu.make_async_copy(table_hbm.at[pl.ds(2 * F, F), pl.ds(0, F)], band, load_sem.at[groups + 1])
    load(0).start()
    load_table.start()
    load_band.start()
    for g in range(1, groups):
        load(g).start()
    make_picker(index_ref, picker, (win, y_peer), rows)
    pl.semaphore_wait(barrier, 2 * line + 2)

    def halo(g, way):
        at = pl.ds(pl.multiple_of(g * gw, gw), gw)
        if way == 0:
            return pltpu.make_async_remote_copy(
                src_ref=traces_hbm.at[pl.ds(0, side), at], dst_ref=nxt.at[:, at], send_sem=halo_send.at[g, 0],
                recv_sem=halo_recv.at[g, 0], device_id={"chan": left}, device_id_type=MESH)
        return pltpu.make_async_remote_copy(
            src_ref=traces_hbm.at[pl.ds(chans - side, side), at], dst_ref=prev.at[:, at], send_sem=halo_send.at[g, 1],
            recv_sem=halo_recv.at[g, 1], device_id={"chan": right}, device_id_type=MESH)

    for g in range(groups):
        for way in range(2):
            halo(g, way).start()
    for d in range(1, line):
        pl.semaphore_signal(
            group_sem, inc=1, device_id={"chan": me // line * line + lax.rem(me + d, line)}, device_id_type=MESH)
    load_table.wait()
    load_band.wait()
    for g in range(groups):
        load(g).wait()

    bins = lax.broadcasted_iota(jnp.int32, (F, 1), 0)
    counts = jnp.minimum(bins + K, F - 1) - jnp.maximum(bins - K, 0) + 1
    per_count = 1.0 / counts.astype(F32)
    lane = lax.broadcasted_iota(jnp.int32, (n, 128), 1)

    def normalise(g, i):
        at = pl.ds(pl.multiple_of(g * gw, gw), gw)
        if i < chans - side:
            low = traces[i, at, :].astype(F32)
            if i + GAUGE < chans:
                high = traces[i + GAUGE, at, :].astype(F32)
            else:
                high = jnp.where(me == n - 1, 0.0, nxt[i + GAUGE - chans, at, :].astype(F32))
        else:
            low = prev[i - chans + side, at, :].astype(F32)
            high = jnp.where(me == 0, 0.0, traces[i - chans + GAUGE, at, :].astype(F32))
        diff = high - low
        scale = lax.rsqrt(jnp.sum(diff * diff, axis=1, keepdims=True) * (1.0 / length) + 1e-05)
        norm_buf[g, pl.ds(i * gw, gw), :] = (diff * scale).astype(BF16)

    def whiten(g, tile):
        normed = norm_buf[g, pl.ds(tile * 128, 128), :]
        re = lax.dot_general(table[pl.ds(0, F), :], normed, NT, preferred_element_type=F32)
        im = lax.dot_general(table[pl.ds(F, F), :], normed, NT, preferred_element_type=F32)
        magnitude = jnp.sqrt(re * re + im * im).astype(BF16)
        smooth = jnp.dot(band[...], magnitude, preferred_element_type=F32) * per_count
        gain = 1.0 / (smooth + 1e-06)
        white = (re * gain, im * gain)
        q = [white[p % 2][(p // 2) * n:(p // 2 + 1) * n] for p in range(8)]
        for bit in range(3):
            step = gw << bit
            upper = (lane // step) % 2 == 1
            fresh = list(q)
            for p in range(8):
                if p & (1 << bit):
                    continue
                a, b = q[p], q[p | (1 << bit)]
                fresh[p] = jnp.where(upper, pltpu.roll(b, step, 1), a)
                fresh[p | (1 << bit)] = jnp.where(upper, b, pltpu.roll(a, 128 - step, 1))
            q = fresh
        for c in range(8):
            mixed[g, pl.ds(tile * 8 + c, n, stride=chans), :] = q[c]

    def before(g, carry):
        for i in range(chans - GAUGE):
            normalise(g, i)
        whiten(g, 0)
        return carry

    lax.fori_loop(0, groups, before, 0)
    pl.semaphore_wait(group_sem, line - 1)
    pl.semaphore_signal(all_sem, inc=1, device_id={"win": y_peer}, device_id_type=MESH)

    def after(g, carry):
        halo(g, 0).wait()
        halo(g, 1).wait()
        for i in range(chans - GAUGE, chans):
            normalise(g, i)
        whiten(g, 1)
        sent[g] = mixed[g].astype(BF16).reshape(n, chans, 128)

        def send(d, c):
            peer = lax.rem(me + 5 * d, n)
            pltpu.make_async_remote_copy(
                src_ref=sent.at[g, peer], dst_ref=held.at[g, me], send_sem=a2a_send.at[g], recv_sem=a2a_recv.at[g],
                device_id={"chan": peer}, device_id_type=MESH).start()
            return c

        lax.fori_loop(1, n, send, 0)
        held[g, me] = sent[g, me]
        return carry

    lax.fori_loop(0, groups, after, 0)

    def all_received(g):
        return pltpu.make_async_remote_copy(
            src_ref=sent.at[g, pl.ds(0, n - 1)], dst_ref=held.at[g, pl.ds(0, n - 1)], send_sem=a2a_send.at[g],
            recv_sem=a2a_recv.at[g], device_id={"chan": right}, device_id_type=MESH)

    def forward(g):
        return pltpu.make_async_remote_copy(
            src_ref=held.at[g], dst_ref=other.at[g], send_sem=core_send.at[g], recv_sem=core_recv.at[g],
            device_id={"win": core_peer}, device_id_type=MESH)

    lane16 = lax.broadcasted_iota(jnp.int32, (16, 128), 1)
    is_im = (lane16 // gw) % 2 == 1
    own_row = lax.broadcasted_iota(jnp.int32, (n, chans, 128), 1) < chans - side

    def straight(block):
        block = block.astype(F32)
        following = jnp.concatenate([block[1:], block[:1]], axis=0)
        return jnp.where(own_row, block, following).reshape(rows, 128).astype(BF16)

    def weights_of(block):
        picked = jnp.dot(picker[...], block, preferred_element_type=F32)
        pieces = []
        for t in range(2):
            pk = picked[t * 16:(t + 1) * 16]
            swapped = jnp.where(is_im, -pltpu.roll(pk, gw, 1), pltpu.roll(pk, 128 - gw, 1))
            for q in range(4):
                mine = (lane16 // (2 * gw)) == q
                pieces.append(jnp.where(mine, pk, 0.0))
                pieces.append(jnp.where(mine, swapped, 0.0))
        return jnp.concatenate(pieces, axis=0).astype(BF16)

    blocks, weights = [], []
    for g in range(groups):
        all_received(g).wait_recv()
        forward(g).start()
        for source in (held, other):
            if source is other:
                forward(g).wait_recv()
            blocks.append(straight(source[g]))
            weights.append(weights_of(blocks[-1]))
        block = jnp.concatenate(blocks[-2:], axis=1)
        weight = jnp.concatenate(weights[-2:], axis=1)
        term = lax.dot_general(block, weight, NT, preferred_element_type=F32)
        if g == 0:
            acc[...] = term
        else:
            acc[...] += term

    part = rows // parts
    per_part = n // parts
    first_peer = me // (n // 4) * (n // 4)

    def base(r):
        return lax.rem(first_peer + r * per_part, n)

    def at(r):
        return pl.ds(pl.multiple_of(base(r) * chans, part), part)

    def y_copy(r):
        return pltpu.make_async_remote_copy(
            src_ref=y_out.at[at(r)], dst_ref=y_in.at[at(r)], send_sem=y_send.at[r], recv_sem=y_recv.at[r],
            device_id={"win": y_peer}, device_id_type=MESH)

    summed = [r for r in range(parts) if r // (parts // 4) % 2 == 1]
    direct = [r for r in range(parts) if r not in summed]
    share = 1.0 / (wins * 4)

    def give(r, source, target, to_win, sems, skip):
        def one(d, c):
            peer = base(r) + lax.rem(me + d, per_part)

            def start():
                pltpu.make_async_remote_copy(
                    src_ref=source.at[peer], dst_ref=target.at[me], send_sem=sems[0], recv_sem=sems[1],
                    device_id={"chan": peer, "win": to_win}, device_id_type=MESH).start()

            if skip:
                pl.when(peer != me)(start)
            else:
                start()
            return c

        lax.fori_loop(0, per_part, one, 0)

    def tiles(value):
        return (value * share).astype(BF16).reshape(per_part, chans, 128)

    for r in summed:
        y_out[at(r), :] = acc[at(r), 128:256].astype(BF16)
        y_copy(r).start()
    pl.semaphore_wait(all_sem, 1)
    for r in direct:
        back_out[pl.ds(base(r), per_part)] = tiles(acc[at(r), 0:128])
        give(r, back_out, back_in, win, (back_send, back_recv), r // (parts // 4) == 0)
        far_out[pl.ds(base(r), per_part)] = tiles(acc[at(r), 128:256])
        give(r, far_out, far_in, y_peer, (far_send, far_recv), False)
    for r in summed:
        y_copy(r).wait_recv()
        back_out[pl.ds(base(r), per_part)] = tiles(acc[at(r), 0:128] + y_in[at(r), :].astype(F32))
        give(r, back_out, back_in, win, (back_send, back_recv), False)
    back_in[me] = back_out[me]

    def all_back(source, target, count, sems):
        return pltpu.make_async_remote_copy(
            src_ref=source.at[pl.ds(0, count)], dst_ref=target.at[pl.ds(0, count)], send_sem=sems[0], recv_sem=sems[1],
            device_id={"chan": right}, device_id_type=MESH)

    back = all_back(back_out, back_in, n - 1, (back_send, back_recv))
    far = all_back(far_out, far_in, n // 2, (far_send, far_recv))
    back.wait_recv()
    far.wait_recv()
    arrange(back_in, far_in, out_ref, back_f32, halves)
    for g in range(groups):
        all_received(g).wait_send()
        forward(g).wait_send()
    for r in summed:
        y_copy(r).wait_send()
    back.wait_send()
    far.wait_send()


def arrange(near, far, out_ref, back_f32, halves):
    n, chans, _ = near.shape
    back_f32[...] = (near[...].astype(F32) + far[...].astype(F32)).reshape(n * chans, 128)
    for c in range(chans):
        flipped = back_f32[pl.ds(c, n, stride=chans), :].T
        for half in range(2):
            both = jnp.concatenate([flipped[half * 64:half * 64 + 32], flipped[half * 64 + 32:half * 64 + 64]], axis=1)
            halves[half, pl.ds(c, 32, stride=chans), :] = both
    out_ref[:, pl.ds(0, 128)] = halves[0]
    out_ref[:, pl.ds(128, 128)] = halves[1]


def solution(mesh):
    n = mesh.shape["chan"]

    def per_device(traces, source_index):
        chans, wins, length = traces.shape
        groups, parts = 3, 16
        gw = wins // groups
        rows = n * chans
        vmem = pl.BlockSpec(memory_space=pltpu.VMEM)
        hbm = pl.BlockSpec(memory_space=pltpu.HBM)
        out = pl.pallas_call(
            functools.partial(body, n, (chans, wins, length, groups, parts)),
            out_shape=jax.ShapeDtypeStruct((2 * 16 * chans, F), F32),
            in_specs=[pl.BlockSpec(memory_space=pltpu.SMEM), hbm, hbm],
            out_specs=vmem,
            scratch_shapes=[
                pltpu.VMEM((chans, wins, length), BF16),
                pltpu.VMEM((2 * F, length), BF16),
                pltpu.VMEM((F, F), BF16),
                pltpu.VMEM((2 * 16, rows), BF16),
                pltpu.SemaphoreType.DMA((groups + 2,)),
                pltpu.VMEM((GAUGE // 2, wins, length), BF16),
                pltpu.VMEM((GAUGE // 2, wins, length), BF16),
                pltpu.VMEM((groups, chans * gw, length), BF16),
                pltpu.VMEM((groups, rows, 128), F32),
                pltpu.VMEM((groups, n, chans, 128), BF16),
                pltpu.VMEM((groups, n, chans, 128), BF16),
                pltpu.VMEM((groups, n, chans, 128), BF16),
                pltpu.VMEM((rows, 256), F32),
                pltpu.VMEM((rows, 128), BF16),
                pltpu.VMEM((rows, 128), BF16),
                pltpu.VMEM((n, chans, 128), BF16),
                pltpu.VMEM((n, chans, 128), BF16),
                pltpu.VMEM((n, chans, 128), BF16),
                pltpu.VMEM((n, chans, 128), BF16),
                pltpu.SemaphoreType.DMA((groups, 2)),
                pltpu.SemaphoreType.DMA((groups, 2)),
                pltpu.SemaphoreType.DMA((groups,)),
                pltpu.SemaphoreType.DMA((groups,)),
                pltpu.SemaphoreType.DMA((groups,)),
                pltpu.SemaphoreType.DMA((groups,)),
                pltpu.SemaphoreType.DMA((parts,)),
                pltpu.SemaphoreType.DMA((parts,)),
                pltpu.SemaphoreType.DMA,
                pltpu.SemaphoreType.DMA,
                pltpu.SemaphoreType.DMA,
                pltpu.SemaphoreType.DMA,
                pltpu.SemaphoreType.REGULAR,
                pltpu.SemaphoreType.REGULAR,
                pltpu.VMEM((rows, 128), F32),
                pltpu.VMEM((2, 2 * 16 * chans, 128), F32),
            ],
            compiler_params=pltpu.CompilerParams(
                collective_id=0, has_side_effects=True, vmem_limit_bytes=52 * 2**20
            ),
        )(source_index, traces, jnp.asarray(make_table(length)))
        return out.reshape(2, 16, chans, F)

    return jax.shard_map(
        per_device,
        mesh=mesh,
        in_specs=(P("chan", "win", None), P()),
        out_specs=P(None, "win", "chan", None),
        check_vma=False,
    )
```

```python
import functools
import math

import jax
import jax.numpy as jnp
import ml_dtypes
import numpy as np
from jax import lax
from jax.experimental import pallas as pl
from jax.experimental.pallas import tpu as pltpu
from jax.sharding import PartitionSpec as P

F = 256
F0 = 1
K = 64
GAUGE = 4
MESH = pl.DeviceIdType.MESH
BF16 = jnp.bfloat16
F32 = jnp.float32
NT = (((1,), (1,)), ((), ()))


def make_table(length):
    times = np.arange(length, dtype=np.int64)[None, :]
    bins = np.arange(F, dtype=np.int64)[:, None] + F0
    phase = (times * bins % length).astype(np.float32) * np.float32(2.0 * math.pi / length)
    phase = phase.astype(np.float64)
    band = np.zeros((F, length))
    band[:, :F] = np.abs(np.arange(F)[:, None] - np.arange(F)[None, :]) <= K
    return np.concatenate([np.cos(phase), -np.sin(phase), band], axis=0).astype(np.float32).astype(ml_dtypes.bfloat16)


def make_picker(index_ref, picker, owners, rows, chans, side):
    sub = lax.broadcasted_iota(jnp.int32, (8, 1), 0)
    column = lax.broadcasted_iota(jnp.int32, (8, rows), 1)
    for t, owner in enumerate(owners):
        tiles = []
        for half in range(2):
            ids = jnp.zeros((8, 1), jnp.int32)
            for r in range(8):
                ids = jnp.where(sub == r, index_ref[owner * 16 + half * 8 + r], ids)
            ids = jnp.where(lax.rem(ids, chans) < chans - side, ids, lax.rem(ids + chans, rows))
            tiles.append((column == ids).astype(F32))
        picker[pl.ds(t * 16, 16), :] = jnp.concatenate(tiles, axis=0).astype(BF16)


def body(n, sizes, index_ref, traces_hbm, table_hbm, out_ref, traces, table, band, picker, load_sem, prev, nxt, norm_buf,
         mixed, sent, held, other, acc, y_out, y_in, back_out, back_in, far_out, far_in, halo_send, halo_recv, a2a_send,
         a2a_recv, core_send, core_recv, y_send, y_recv, back_send, back_recv, far_send,
         far_recv, group_sem, all_sem, back_f32, halves):
    chans, wins, length, groups, parts = sizes
    side = GAUGE // 2
    gw = wins // groups
    rows = n * chans
    me = lax.axis_index("chan")
    win = lax.axis_index("win")
    core_peer = win + 1 - 2 * lax.rem(win, 2)
    y_peer = lax.rem(win + 2, 4)
    right, left = lax.rem(me + 1, n), lax.rem(me + n - 1, n)

    barrier = pltpu.get_barrier_semaphore()

    line = 8
    far_in[...] = jnp.zeros_like(far_in)
    for d in range(1, line):
        pl.semaphore_signal(
            barrier, inc=1, device_id={"chan": me // line * line + lax.rem(me + d, line)}, device_id_type=MESH)
        pl.semaphore_signal(barrier, inc=1, device_id={"chan": lax.rem(me + line * d, n)}, device_id_type=MESH)
    for peer in (left, right):
        pl.semaphore_signal(barrier, inc=1, device_id={"chan": peer}, device_id_type=MESH)
    for peer in (core_peer, y_peer):
        pl.semaphore_signal(barrier, inc=1, device_id={"win": peer}, device_id_type=MESH)

    def load(g):
        at = pl.ds(g * gw, gw)
        return pltpu.make_async_copy(traces_hbm.at[:, at], traces.at[:, at], load_sem.at[g])

    load_table = pltpu.make_async_copy(table_hbm.at[pl.ds(0, 2 * F)], table, load_sem.at[groups])
    load_band = pltpu.make_async_copy(table_hbm.at[pl.ds(2 * F, F), pl.ds(0, F)], band, load_sem.at[groups + 1])
    load(0).start()
    load_table.start()
    load_band.start()
    for g in range(1, groups):
        load(g).start()
    make_picker(index_ref, picker, (win, y_peer), rows, chans, side)
    pl.semaphore_wait(barrier, 2 * line + 2)

    def halo(g, way):
        at = pl.ds(pl.multiple_of(g * gw, gw), gw)
        if way == 0:
            return pltpu.make_async_remote_copy(
                src_ref=traces_hbm.at[pl.ds(0, side), at], dst_ref=nxt.at[:, at], send_sem=halo_send.at[g, 0],
                recv_sem=halo_recv.at[g, 0], device_id={"chan": left}, device_id_type=MESH)
        return pltpu.make_async_remote_copy(
            src_ref=traces_hbm.at[pl.ds(chans - side, side), at], dst_ref=prev.at[:, at], send_sem=halo_send.at[g, 1],
            recv_sem=halo_recv.at[g, 1], device_id={"chan": right}, device_id_type=MESH)

    for g in range(groups):
        for way in range(2):
            halo(g, way).start()
    for d in range(1, line):
        pl.semaphore_signal(
            group_sem, inc=1, device_id={"chan": me // line * line + lax.rem(me + d, line)}, device_id_type=MESH)
    load_table.wait()
    load_band.wait()
    for g in range(groups):
        load(g).wait()

    bins = lax.broadcasted_iota(jnp.int32, (F, 1), 0)
    counts = jnp.minimum(bins + K, F - 1) - jnp.maximum(bins - K, 0) + 1
    per_count = 1.0 / counts.astype(F32)
    lane = lax.broadcasted_iota(jnp.int32, (n, 128), 1)

    def normalise(g, i):
        at = pl.ds(pl.multiple_of(g * gw, gw), gw)
        if i < chans - side:
            low = traces[i, at, :].astype(F32)
            if i + GAUGE < chans:
                high = traces[i + GAUGE, at, :].astype(F32)
            else:
                high = jnp.where(me == n - 1, 0.0, nxt[i + GAUGE - chans, at, :].astype(F32))
        else:
            low = prev[i - chans + side, at, :].astype(F32)
            high = jnp.where(me == 0, 0.0, traces[i - chans + GAUGE, at, :].astype(F32))
        diff = high - low
        scale = lax.rsqrt(jnp.sum(diff * diff, axis=1, keepdims=True) * (1.0 / length) + 1e-05)
        norm_buf[g, pl.ds(i * gw, gw), :] = (diff * scale).astype(BF16)

    def whiten(g, tile):
        normed = norm_buf[g, pl.ds(tile * 128, 128), :]
        re = lax.dot_general(table[pl.ds(0, F), :], normed, NT, preferred_element_type=F32)
        im = lax.dot_general(table[pl.ds(F, F), :], normed, NT, preferred_element_type=F32)
        magnitude = jnp.sqrt(re * re + im * im).astype(BF16)
        smooth = jnp.dot(band[...], magnitude, preferred_element_type=F32) * per_count
        gain = 1.0 / (smooth + 1e-06)
        white = (re * gain, im * gain)
        q = [white[p % 2][(p // 2) * n:(p // 2 + 1) * n] for p in range(8)]
        for bit in range(3):
            step = gw << bit
            upper = (lane // step) % 2 == 1
            fresh = list(q)
            for p in range(8):
                if p & (1 << bit):
                    continue
                a, b = q[p], q[p | (1 << bit)]
                fresh[p] = jnp.where(upper, pltpu.roll(b, step, 1), a)
                fresh[p | (1 << bit)] = jnp.where(upper, b, pltpu.roll(a, 128 - step, 1))
            q = fresh
        for c in range(8):
            mixed[g, pl.ds(tile * 8 + c, n, stride=chans), :] = q[c]

    def before(g, carry):
        for i in range(chans - GAUGE):
            normalise(g, i)
        whiten(g, 0)
        return carry

    lax.fori_loop(0, groups, before, 0)
    pl.semaphore_wait(group_sem, line - 1)
    pl.semaphore_signal(all_sem, inc=1, device_id={"win": y_peer}, device_id_type=MESH)

    def after(g, carry):
        halo(g, 0).wait()
        halo(g, 1).wait()
        for i in range(chans - GAUGE, chans):
            normalise(g, i)
        whiten(g, 1)
        sent[g] = mixed[g].astype(BF16).reshape(n, chans, 128)

        def send(d, c):
            peer = lax.rem(me + 5 * d, n)
            pltpu.make_async_remote_copy(
                src_ref=sent.at[g, peer], dst_ref=held.at[g, me], send_sem=a2a_send.at[g], recv_sem=a2a_recv.at[g],
                device_id={"chan": peer}, device_id_type=MESH).start()
            return c

        lax.fori_loop(1, n, send, 0, unroll=9)
        held[g, me] = sent[g, me]
        return carry

    lax.fori_loop(0, groups, after, 0)

    def all_received(g):
        return pltpu.make_async_remote_copy(
            src_ref=sent.at[g, pl.ds(0, n - 1)], dst_ref=held.at[g, pl.ds(0, n - 1)], send_sem=a2a_send.at[g],
            recv_sem=a2a_recv.at[g], device_id={"chan": right}, device_id_type=MESH)

    def forward(g):
        return pltpu.make_async_remote_copy(
            src_ref=held.at[g], dst_ref=other.at[g], send_sem=core_send.at[g], recv_sem=core_recv.at[g],
            device_id={"win": core_peer}, device_id_type=MESH)

    lane16 = lax.broadcasted_iota(jnp.int32, (16, 128), 1)
    is_im = (lane16 // gw) % 2 == 1
    own_row = lax.broadcasted_iota(jnp.int32, (n, chans, 128), 1) < chans - side

    def straight(block):
        following = jnp.concatenate([block[1:], block[:1]], axis=0)
        return jnp.where(own_row, block, following).reshape(rows, 128)

    def weights_of(block):
        picked = jnp.dot(picker[...], block, preferred_element_type=F32)
        pieces = []
        for t in range(2):
            pk = picked[t * 16:(t + 1) * 16]
            swapped = jnp.where(is_im, -pltpu.roll(pk, gw, 1), pltpu.roll(pk, 128 - gw, 1))
            for q in range(4):
                mine = (lane16 // (2 * gw)) == q
                pieces.append(jnp.where(mine, pk, 0.0))
                pieces.append(jnp.where(mine, swapped, 0.0))
        return jnp.concatenate(pieces, axis=0).astype(BF16)

    blocks, weights = [], []
    for g in range(groups):
        all_received(g).wait_recv()
        forward(g).start()
        for source in (held, other):
            if source is other:
                forward(g).wait_recv()
            blocks.append(straight(source[g]))
            weights.append(weights_of(source[g].reshape(rows, 128)))
        block = jnp.concatenate(blocks[-2:], axis=1)
        weight = jnp.concatenate(weights[-2:], axis=1)
        term = lax.dot_general(block, weight, NT, preferred_element_type=F32)
        if g == 0:
            acc[...] = term
        else:
            acc[...] += term

    part = rows // parts
    per_part = n // parts
    first_peer = me // (n // 4) * (n // 4)

    def base(r):
        return lax.rem(first_peer + r * per_part, n)

    def at(r):
        return pl.ds(pl.multiple_of(base(r) * chans, part), part)

    def y_copy(r):
        return pltpu.make_async_remote_copy(
            src_ref=y_out.at[at(r)], dst_ref=y_in.at[at(r)], send_sem=y_send.at[r], recv_sem=y_recv.at[r],
            device_id={"win": y_peer}, device_id_type=MESH)

    summed = [r for r in range(parts) if r // (parts // 4) % 2 == 1]
    direct = [r for r in range(parts) if r not in summed]
    share = 1.0 / (wins * 4)

    def give(r, source, target, to_win, sems, skip):
        def one(d, c):
            peer = base(r) + lax.rem(me + d, per_part)

            def start():
                pltpu.make_async_remote_copy(
                    src_ref=source.at[peer], dst_ref=target.at[me], send_sem=sems[0], recv_sem=sems[1],
                    device_id={"chan": peer, "win": to_win}, device_id_type=MESH).start()

            if skip:
                pl.when(peer != me)(start)
            else:
                start()
            return c

        lax.fori_loop(0, per_part, one, 0, unroll=True)

    def tiles(value):
        return (value * share).astype(BF16).reshape(per_part, chans, 128)

    for r in summed:
        y_out[at(r), :] = acc[at(r), 128:256].astype(BF16)
        y_copy(r).start()
    pl.semaphore_wait(all_sem, 1)
    for r in direct:
        back_out[pl.ds(base(r), per_part)] = tiles(acc[at(r), 0:128])
        give(r, back_out, back_in, win, (back_send, back_recv), r // (parts // 4) == 0)
        far_out[pl.ds(base(r), per_part)] = tiles(acc[at(r), 128:256])
        give(r, far_out, far_in, y_peer, (far_send, far_recv), False)
    for r in summed:
        y_copy(r).wait_recv()
        back_out[pl.ds(base(r), per_part)] = tiles(acc[at(r), 0:128] + y_in[at(r), :].astype(F32))
        give(r, back_out, back_in, win, (back_send, back_recv), False)
    back_in[me] = back_out[me]

    def all_back(source, target, count, sems):
        return pltpu.make_async_remote_copy(
            src_ref=source.at[pl.ds(0, count)], dst_ref=target.at[pl.ds(0, count)], send_sem=sems[0], recv_sem=sems[1],
            device_id={"chan": right}, device_id_type=MESH)

    back = all_back(back_out, back_in, n - 1, (back_send, back_recv))
    far = all_back(far_out, far_in, n // 2, (far_send, far_recv))
    back.wait_recv()
    far.wait_recv()
    arrange(back_in, far_in, out_ref, back_f32, halves)
    for g in range(groups):
        all_received(g).wait_send()
        forward(g).wait_send()
    for r in summed:
        y_copy(r).wait_send()
    back.wait_send()
    far.wait_send()


def arrange(near, far, out_ref, back_f32, halves):
    n, chans, _ = near.shape
    back_f32[...] = (near[...].astype(F32) + far[...].astype(F32)).reshape(n * chans, 128)
    for c in range(chans):
        flipped = back_f32[pl.ds(c, n, stride=chans), :].T
        for half in range(2):
            both = jnp.concatenate([flipped[half * 64:half * 64 + 32], flipped[half * 64 + 32:half * 64 + 64]], axis=1)
            halves[half, pl.ds(c, 32, stride=chans), :] = both
    out_ref[:, pl.ds(0, 128)] = halves[0]
    out_ref[:, pl.ds(128, 128)] = halves[1]


def solution(mesh):
    n = mesh.shape["chan"]

    def per_device(traces, source_index):
        chans, wins, length = traces.shape
        groups, parts = 3, 16
        gw = wins // groups
        rows = n * chans
        vmem = pl.BlockSpec(memory_space=pltpu.VMEM)
        hbm = pl.BlockSpec(memory_space=pltpu.HBM)
        out = pl.pallas_call(
            functools.partial(body, n, (chans, wins, length, groups, parts)),
            out_shape=jax.ShapeDtypeStruct((2 * 16 * chans, F), F32),
            in_specs=[pl.BlockSpec(memory_space=pltpu.SMEM), hbm, hbm],
            out_specs=vmem,
            scratch_shapes=[
                pltpu.VMEM((chans, wins, length), BF16),
                pltpu.VMEM((2 * F, length), BF16),
                pltpu.VMEM((F, F), BF16),
                pltpu.VMEM((2 * 16, rows), BF16),
                pltpu.SemaphoreType.DMA((groups + 2,)),
                pltpu.VMEM((GAUGE // 2, wins, length), BF16),
                pltpu.VMEM((GAUGE // 2, wins, length), BF16),
                pltpu.VMEM((groups, chans * gw, length), BF16),
                pltpu.VMEM((groups, rows, 128), F32),
                pltpu.VMEM((groups, n, chans, 128), BF16),
                pltpu.VMEM((groups, n, chans, 128), BF16),
                pltpu.VMEM((groups, n, chans, 128), BF16),
                pltpu.VMEM((rows, 256), F32),
                pltpu.VMEM((rows, 128), BF16),
                pltpu.VMEM((rows, 128), BF16),
                pltpu.VMEM((n, chans, 128), BF16),
                pltpu.VMEM((n, chans, 128), BF16),
                pltpu.VMEM((n, chans, 128), BF16),
                pltpu.VMEM((n, chans, 128), BF16),
                pltpu.SemaphoreType.DMA((groups, 2)),
                pltpu.SemaphoreType.DMA((groups, 2)),
                pltpu.SemaphoreType.DMA((groups,)),
                pltpu.SemaphoreType.DMA((groups,)),
                pltpu.SemaphoreType.DMA((groups,)),
                pltpu.SemaphoreType.DMA((groups,)),
                pltpu.SemaphoreType.DMA((parts,)),
                pltpu.SemaphoreType.DMA((parts,)),
                pltpu.SemaphoreType.DMA,
                pltpu.SemaphoreType.DMA,
                pltpu.SemaphoreType.DMA,
                pltpu.SemaphoreType.DMA,
                pltpu.SemaphoreType.REGULAR,
                pltpu.SemaphoreType.REGULAR,
                pltpu.VMEM((rows, 128), F32),
                pltpu.VMEM((2, 2 * 16 * chans, 128), F32),
            ],
            compiler_params=pltpu.CompilerParams(
                collective_id=0, has_side_effects=True, vmem_limit_bytes=52 * 2**20
            ),
        )(source_index, traces, jnp.asarray(make_table(length)))
        return out.reshape(2, 16, chans, F)

    return jax.shard_map(
        per_device,
        mesh=mesh,
        in_specs=(P("chan", "win", None), P()),
        out_specs=P(None, "win", "chan", None),
        check_vma=False,
    )
```
